32 devices in a mesh: gx: 16 (over z, x, core), gy: 2 (over y).
Axes of the slice: x: 2, y: 2, z: 4, core: 2. Of those that a mesh axis runs over, the one named last changes fastest.
Arguments:
- source: float32 [64, 64, 256], P('gx', 'gy'), may hold values from -6 to 6
- labels: int32 [64, 64, 256], P('gx', 'gy'), may hold values from 0 to 1, as said below
- jitter: float32 [64, 64, 256], P('gx', 'gy'), may hold values from 0.5 to 2
- phase_sigma: float32 [2], replicated, may hold values from 0.3 to 3
Outputs:
- potential_fine: float32 [64, 64, 256], P('gx', 'gy')
- potential_mid: float32 [32, 32, 128], P('gx', 'gy')
- potential_coarse: float32 [16, 16, 64], P('gx', 'gy')
The draws below stay inside these ranges and needn't reach their ends.
Inputs may be any that keep to these rules, and one draw needn't show every extreme that they name: `labels`: 1 marks cells inside the droplets, 0 the surrounding fluid.
All inputs are finite; a program needn't handle non-finite values.
Results may differ from the reference program's by a relative error of at most 0.0001.
Values sent between devices are 32-bit elements; how exact they have to be, the bound alone decides.
A program may use at most 64 MiB of HBM per device.

```python
import math
import jax
import jax.numpy as jnp
from jax import lax

NZ = 256
SWEEPS = 2
COARSE_SWEEPS = 8
NX = 64
NY = 64


def draw_source(key, part):
    key = jax.random.fold_in(key, 5)
    shape = (NX, NY, NZ)
    values = jnp.clip(jax.random.normal(key, shape, jnp.float32), -6.0, 6.0)
    return values.astype(jnp.float32)


def draw_labels(key, part):
    key = jax.random.fold_in(key, 11)
    subkeys = jax.random.split(key, 4)
    droplets = 6
    shape = (NX, NY, NZ)
    centre_x = jax.random.randint(subkeys[0], (droplets,), 0, NX)
    centre_y = jax.random.randint(subkeys[1], (droplets,), 0, NY)
    centre_z = jax.random.randint(subkeys[2], (droplets,), 0, NZ)
    radius = jax.random.randint(subkeys[3], (droplets,), max(NX // 16, 1), max(NX // 6, 2))
    along_x = lax.broadcasted_iota(jnp.int32, shape, 0)
    along_y = lax.broadcasted_iota(jnp.int32, shape, 1)
    along_z = lax.broadcasted_iota(jnp.int32, shape, 2)
    inside = jnp.zeros(shape, jnp.int32)
    for member in range(droplets):
        distance = (along_x - centre_x[member]) ** 2 + (along_y - centre_y[member]) ** 2 + (along_z - centre_z[member]) ** 2
        inside = jnp.maximum(inside, (distance <= radius[member] ** 2).astype(jnp.int32))
    return inside


def shard_levels(stream_key, extent, cuts, smallest, largest):
    loudness, own = 1.0, jax.random.fold_in(stream_key, 6)
    for position, blocks in cuts:
        steps = jnp.exp(jax.random.uniform(jax.random.fold_in(own, position), (blocks,), jnp.float32, smallest / len(cuts), largest / len(cuts)))
        loudness = loudness * jnp.repeat(steps, extent[position] // blocks).reshape([-1 if axis == position else 1 for axis in range(len(extent))])
    return loudness


def setup_inputs(seed: int = 0) -> dict:
    key_list = jax.random.split(jax.random.key(seed), 5)
    return {
        "source": draw_source(jax.random.fold_in(key_list[4], 71), 0),
        "labels": draw_labels(jax.random.fold_in(key_list[4], 71), 0),
        "jitter": jnp.clip(jnp.exp(math.log(2.0) - 1.3862944 * jax.random.uniform(key_list[2], (NX, NY, NZ), jnp.float32) ** shard_levels(key_list[2], (NX, NY, NZ), ((0, 16), (1, 2)), -0.2, 0.2)), 0.5, 2.0),
        "phase_sigma": jnp.clip(jnp.exp(jax.random.uniform(key_list[3], (2,), jnp.float32, math.log(0.3), math.log(3.0))), 0.3, 3.0),
    }


def neighbours(padded):
    return [padded[2:, 1:-1, 1:-1], padded[:-2, 1:-1, 1:-1], padded[1:-1, 2:, 1:-1],
            padded[1:-1, :-2, 1:-1], padded[1:-1, 1:-1, 2:], padded[1:-1, 1:-1, :-2]]


def weights(padded_sigma):
    centre = padded_sigma[1:-1, 1:-1, 1:-1]
    face_weights = [2.0 * centre * opposite / (centre + opposite) for opposite in neighbours(padded_sigma)]
    diagonal = face_weights[0] + face_weights[1] + face_weights[2] + face_weights[3] + face_weights[4] + face_weights[5]
    return face_weights, diagonal


def linked(padded_field, face_weights):
    others = neighbours(padded_field)
    summed = face_weights[0] * others[0]
    for index_face in range(1, 6):
        summed = summed + face_weights[index_face] * others[index_face]
    return summed


def parity(shape, start_x, start_y):
    index_sum = lax.broadcasted_iota(jnp.int32, shape, 0) + start_x
    index_sum = index_sum + lax.broadcasted_iota(jnp.int32, shape, 1) + start_y
    index_sum = index_sum + lax.broadcasted_iota(jnp.int32, shape, 2)
    return index_sum % 2 == 0


def coarsen(values):
    extent_x, extent_y, extent_z = values.shape
    blocks = values.reshape(extent_x // 2, 2, extent_y // 2, 2, extent_z // 2, 2)
    return blocks.mean(axis=(1, 3, 5))


def smooth(source_term, face_weights, diagonal, factor, red_cells, sweeps):
    potential = jnp.where(red_cells, source_term * factor / diagonal, 0.0)
    potential = jnp.where(red_cells, potential, (source_term * factor + linked(jnp.pad(potential, 1), face_weights)) / diagonal)
    for repeat in range(sweeps - 1):
        potential = jnp.where(red_cells, (source_term * factor + linked(jnp.pad(potential, 1), face_weights)) / diagonal, potential)
        potential = jnp.where(red_cells, potential, (source_term * factor + linked(jnp.pad(potential, 1), face_weights)) / diagonal)
    return potential


def reference(source, labels, jitter, phase_sigma):
    conductivity = jnp.where(labels == 1, phase_sigma[1], phase_sigma[0]) * jitter
    source_term = source
    results = []
    for grid_level in range(3):
        factor = 4.0 ** grid_level
        face_weights, diagonal = weights(jnp.pad(conductivity, 1, mode="edge"))
        red_cells = parity(conductivity.shape, 0, 0)
        sweeps = SWEEPS if grid_level < 2 else COARSE_SWEEPS
        potential = smooth(source_term, face_weights, diagonal, factor, red_cells, sweeps)
        results.append(potential)
        if grid_level < 2:
            remainder = source_term - (diagonal * potential - linked(jnp.pad(potential, 1), face_weights)) / factor
            source_term = coarsen(remainder)
            conductivity = coarsen(conductivity)
    potential_fine = results[0]
    potential_mid = results[1]
    potential_coarse = results[2]
    return (potential_fine, potential_mid, potential_coarse)
```

```python
import functools
import jax
import jax.numpy as jnp
from jax import lax
from jax.experimental import pallas as pl
from jax.experimental.pallas import tpu as pltpu
from jax.sharding import PartitionSpec as P

SWEEPS = 2
COARSE_SWEEPS = 8
PAD = 8
LANES = 128
STEPS = 5
MESH = pl.DeviceIdType.MESH


def pair_matrix(rows, columns):
    row = lax.broadcasted_iota(jnp.int32, (rows, columns), 0)
    column = lax.broadcasted_iota(jnp.int32, (rows, columns), 1)
    return jnp.where(lax.div(row, 2) == lax.rem(column, rows // 2), 0.125, 0.0).astype(jnp.float32)


def coarsen(values, tmp):
    extent_x, extent_y, extent_z = values.shape
    paired = values.reshape(extent_x // 2, 2, extent_y, extent_z)
    paired = (paired[:, 0] + paired[:, 1]).reshape(extent_x // 2 * extent_y, extent_z)
    paired = jnp.dot(
        paired, pair_matrix(extent_z, LANES), precision=lax.Precision.HIGHEST,
        preferred_element_type=jnp.float32,
    )
    rows = extent_x // 2 * extent_y
    tmp[pl.ds(0, rows), :] = paired
    summed = tmp[pl.ds(0, rows // 2, stride=2), :] + tmp[pl.ds(1, rows // 2, stride=2), :]
    return summed.reshape(extent_x // 2, extent_y // 2, LANES)


def iota(shape, dim):
    return lax.broadcasted_iota(jnp.int32, shape, dim)


def make_coeffs(out, rows, centre, others, edges, factor, source):
    face_weights = [
        jnp.where(edge, centre, 2.0 * centre * other / (centre + other))
        for other, edge in zip(others, edges)
    ]
    diagonal = face_weights[0]
    for weight in face_weights[1:]:
        diagonal = diagonal + weight
    inverse = 1.0 / diagonal
    for face in range(6):
        out[face, rows] = jnp.where(edges[face], 0.0, face_weights[face] * inverse)
    out[6, rows] = factor * inverse


def linked(coeffs, rows, others):
    summed = coeffs[0, rows] * others[0]
    for face in range(1, 6):
        summed = summed + coeffs[face, rows] * others[face]
    return summed


class Level:
    def __init__(self, ref, coeffs, halos, sems, counts, extent_z, factor):
        self.ref, self.coeffs = ref, coeffs
        self.xlo, self.xhi, self.ylo, self.yhi = halos
        self.send, self.recv = sems
        self.nx = ref.shape[1]
        self.ny = ref.shape[2] - 2 * PAD
        self.nz = ref.shape[3]
        self.factor = factor
        self.ngx, self.ngy = counts
        self.gx, self.gy = lax.axis_index("gx"), lax.axis_index("gy")

    def copies(self, step):
        kind = 0 if step == 0 else 1
        ref, ny = self.ref.at[kind], self.ny
        ends = [
            (ref.at[0, pl.ds(PAD, ny)], self.xhi, {"gx": self.gx - 1}),
            (ref.at[self.nx - 1, pl.ds(PAD, ny)], self.xlo, {"gx": self.gx + 1}),
            (ref.at[:, pl.ds(PAD, 8)], self.yhi, {"gy": self.gy - 1}),
            (ref.at[:, pl.ds(PAD + ny - 8, 8)], self.ylo, {"gy": self.gy + 1}),
        ]
        return [
            pltpu.make_async_remote_copy(
                src_ref=src, dst_ref=dst.at[step], send_sem=self.send.at[step, place],
                recv_sem=self.recv.at[step, place], device_id=device, device_id_type=MESH,
            )
            for place, (src, dst, device) in enumerate(ends)
        ]

    def sides(self):
        return [
            self.gx > 0, self.gx < self.ngx - 1, self.gy > 0, self.gy < self.ngy - 1,
        ]

    def clear(self):
        for there, buf in zip(self.sides(), (self.xlo, self.xhi, self.ylo, self.yhi)):
            @pl.when(jnp.logical_not(there))
            def _():
                buf[...] = jnp.zeros_like(buf)

    def start(self, step):
        copies = self.copies(step)
        for place in (2, 3, 0, 1):
            pl.when(self.sides()[place])(copies[place].start)

    def wait(self, step):
        copies = self.copies(step)
        opposite = (1, 0, 3, 2)
        for place in range(4):
            @pl.when(self.sides()[place])
            def _():
                copies[place].wait_send()
                copies[opposite[place]].wait_recv()
        kind = 0 if step == 0 else 1
        self.ref[kind, :, pl.ds(PAD - 1, 1), :] = self.ylo[step, :, 7:8, :]
        self.ref[kind, :, pl.ds(PAD + self.ny, 1), :] = self.yhi[step, :, 0:1, :]

    def others(self, step):
        kind = 0 if step == 0 else 1
        ref, ny, nz = self.ref.at[kind], self.ny, self.nz
        centre = ref[:, pl.ds(PAD, ny), :]
        above = jnp.concatenate([centre[1:], self.xhi[step][None]], axis=0)
        below = jnp.concatenate([self.xlo[step][None], centre[:-1]], axis=0)
        return centre, [
            above, below,
            ref[:, pl.ds(PAD + 1, ny), :], ref[:, pl.ds(PAD - 1, ny), :],
            pltpu.roll(centre, nz - 1, 2), pltpu.roll(centre, 1, 2),
        ]

    def weigh(self):
        centre, others = self.others(0)
        shape = centre.shape
        at_x, at_y, at_z = (iota(shape, dim) for dim in range(3))
        at_x, at_y = at_x + self.gx * self.nx, at_y + self.gy * self.ny
        edges = [
            at_x == self.ngx * self.nx - 1, at_x == 0, at_y == self.ngy * self.ny - 1, at_y == 0,
            at_z == self.nz - 1, at_z == 0,
        ]
        make_coeffs(self.coeffs, slice(None), centre, others, edges, self.factor, None)

    def colour(self):
        shape = (self.nx, self.ny, self.nz)
        total = iota(shape, 0) + iota(shape, 1) + iota(shape, 2)
        return lax.rem(total + self.gx * self.nx + self.gy * self.ny, 2) == 0

    def smooth(self, source, beside):
        rows = slice(None)
        coeffs, own = self.coeffs, (1, slice(None), pl.ds(PAD, self.ny))
        right = source * coeffs[6, rows]
        self.right[...] = right
        self.ref[own] = jnp.where(self.colour(), right, 0.0)
        for step in range(1, STEPS):
            self.start(step)
            if step - 1 < len(beside):
                beside[step - 1]()
            self.wait(step)
            centre, others = self.others(step)
            fresh = self.right[...] + linked(coeffs, rows, others)
            if step < STEPS - 1:
                red = self.colour()
                turn = red if step % 2 == 0 else jnp.logical_not(red)
                self.ref[own] = jnp.where(turn, fresh, centre)
            else:
                return (fresh - centre) / coeffs[6, rows]


def kernel(ngx, ngy, src, lab, jit, phase, out0, out1, out2,
           f0, c0, r0, xl0, xh0, yl0, yh0, s0, v0,
           f1, c1, r1, xl1, xh1, yl1, yh1, s1, v1,
           tmp, block, grid, c2, gsend, grecv):
    gx, gy = lax.axis_index("gx"), lax.axis_index("gy")
    me, count = gx * ngy + gy, ngx * ngy
    fine = Level(f0, c0, (xl0, xh0, yl0, yh0), (s0, v0), (ngx, ngy), src.shape[2], 1.0)
    mid = Level(f1, c1, (xl1, xh1, yl1, yh1), (s1, v1), (ngx, ngy), src.shape[2] // 2, 4.0)
    fine.right, mid.right = r0, r1
    nx2, ny2 = block.shape[1], block.shape[2]
    big_x, big_y = ngx * nx2, ngy * ny2
    deep = src.shape[2] // 4

    fine.clear()
    mid.clear()
    grid[...] = jnp.zeros_like(grid)

    def target(offset):
        other = lax.rem(me + offset, count)
        return (lax.div(other, ngy), lax.rem(other, ngy))

    barrier = pltpu.get_barrier_semaphore()

    def greet(offset, carry):
        pl.semaphore_signal(barrier, inc=1, device_id=target(offset), device_id_type=MESH)
        return carry

    lax.fori_loop(1, count, greet, 0)

    sigma = jnp.where(lab[...] == 1, phase[1], phase[0]) * jit[...]
    fine.ref[0, :, pl.ds(PAD, fine.ny), :] = sigma
    f0[1, :, pl.ds(0, PAD), :] = jnp.zeros((fine.nx, PAD, fine.nz), jnp.float32)
    pl.semaphore_wait(barrier, count - 1)
    fine.start(0)

    def place(kind, x, y):
        return grid.at[kind, pl.ds(1 + x * nx2, nx2), pl.ds(pl.multiple_of(PAD + y * ny2, 8), ny2)]

    def gather_copy(kind, offset, sender):
        return pltpu.make_async_remote_copy(
            src_ref=block.at[kind], dst_ref=place(kind, gx, gy), send_sem=gsend.at[kind, offset],
            recv_sem=grecv.at[kind, sender], device_id=target(offset), device_id_type=MESH,
        )

    def gather_start(kind, values):
        block[kind] = values
        place(kind, gx, gy)[...] = values

        def push(offset, carry):
            gather_copy(kind, offset, me).start()
            return carry

        lax.fori_loop(1, count, push, 0)

    def gather_wait(kind):
        def pull(offset, carry):
            copy = gather_copy(kind, offset, lax.rem(me + offset, count))
            copy.wait_send()
            copy.wait_recv()
            return carry

        lax.fori_loop(1, count, pull, 0)

    sigma1 = coarsen(sigma, tmp)
    mid.ref[0, :, pl.ds(PAD, mid.ny), :] = sigma1
    mid.start(0)
    gather_start(0, coarsen(sigma1, tmp))
    fine.wait(0)
    fine.weigh()

    def mid_weights():
        mid.wait(0)
        mid.weigh()

    chunk = min(big_x, 16)
    rows_y = pl.ds(PAD, big_y)

    def chunks(body):
        if big_x == chunk:
            body(0)
        else:
            def step(index, carry):
                body(index * chunk)
                return carry
            lax.fori_loop(0, big_x // chunk, step, 0)

    def grid_others(kind, first):
        ref = grid.at[kind]
        here = pl.ds(1 + first, chunk)
        centre = ref[here, rows_y, :]
        return centre, [
            ref[pl.ds(2 + first, chunk), rows_y, :], ref[pl.ds(first, chunk), rows_y, :],
            ref[here, pl.ds(PAD + 1, big_y), :], ref[here, pl.ds(PAD - 1, big_y), :],
            pltpu.roll(centre, LANES - 1, 2), pltpu.roll(centre, 1, 2),
        ]

    def coarse_weights():
        gather_wait(0)

        def weigh(first):
            centre, others = grid_others(0, first)
            shape = centre.shape
            at_x, at_y, at_z = (iota(shape, dim) for dim in range(3))
            at_x = at_x + first
            edges = [
                at_x == big_x - 1, at_x == 0, at_y == big_y - 1, at_y == 0,
                lax.rem(at_z, deep) == deep - 1, lax.rem(at_z, deep) == 0,
            ]
            make_coeffs(c2, pl.ds(first, chunk), centre, others, edges, 16.0, None)

        chunks(weigh)

    remainder = fine.smooth(src[...], [mid_weights, coarse_weights])
    source1 = coarsen(remainder, tmp)

    def write_fine():
        out0[...] = f0[1, :, pl.ds(PAD, fine.ny), :]

    remainder = mid.smooth(source1, [write_fine])
    gather_start(1, coarsen(remainder, tmp))
    out1[...] = f1[1, :, pl.ds(PAD, mid.ny), :]
    gather_wait(1)

    def colour(first):
        shape = (chunk, big_y, LANES)
        return lax.rem(iota(shape, 0) + iota(shape, 1) + iota(shape, 2) + first, 2) == 0

    def first_red(first):
        here = pl.ds(first, chunk)
        right = grid[1, pl.ds(1 + first, chunk), rows_y, :] * c2[6, here]
        c2[7, here] = right
        grid[2, pl.ds(1 + first, chunk), rows_y, :] = jnp.where(colour(first), right, 0.0)

    def half(parity):
        def body(first):
            here = pl.ds(first, chunk)
            centre, others = grid_others(2, first)
            fresh = c2[7, here] + linked(c2, here, others)
            red = colour(first)
            turn = red if parity == 0 else jnp.logical_not(red)
            grid[2, pl.ds(1 + first, chunk), rows_y, :] = jnp.where(turn, fresh, centre)
        chunks(body)

    chunks(first_red)
    half(1)

    def sweep(repeat, carry):
        half(0)
        half(1)
        return carry

    lax.fori_loop(0, COARSE_SWEEPS - 1, sweep, 0)
    mine = place(2, gx, gy)[...]
    out2[...] = mine[:, :, :deep]


def per_device(ngx, ngy, source, labels, jitter, phase_sigma):
    nx, ny, nz = source.shape
    count = ngx * ngy
    f32 = jnp.float32

    def level(nx, ny, nz):
        return [
            pltpu.VMEM((2, nx, ny + 2 * PAD, nz), f32),
            pltpu.VMEM((7, nx, ny, nz), f32),
            pltpu.VMEM((nx, ny, nz), f32),
            pltpu.VMEM((STEPS, ny, nz), f32),
            pltpu.VMEM((STEPS, ny, nz), f32),
            pltpu.VMEM((STEPS, nx, 8, nz), f32),
            pltpu.VMEM((STEPS, nx, 8, nz), f32),
            pltpu.SemaphoreType.DMA((STEPS, 4)),
            pltpu.SemaphoreType.DMA((STEPS, 4)),
        ]

    nx2, ny2 = nx // 4, ny // 4
    vmem = pl.BlockSpec(memory_space=pltpu.VMEM)
    return pl.pallas_call(
        functools.partial(kernel, ngx, ngy),
        out_shape=(
            jax.ShapeDtypeStruct((nx, ny, nz), f32),
            jax.ShapeDtypeStruct((nx // 2, ny // 2, nz // 2), f32),
            jax.ShapeDtypeStruct((nx2, ny2, nz // 4), f32),
        ),
        in_specs=[vmem, vmem, vmem, pl.BlockSpec(memory_space=pltpu.SMEM)],
        out_specs=(vmem, vmem, vmem),
        scratch_shapes=level(nx, ny, nz) + level(nx // 2, ny // 2, nz // 2) + [
            pltpu.VMEM((nx // 2 * ny, LANES), f32),
            pltpu.VMEM((2, nx2, ny2, LANES), f32),
            pltpu.VMEM((3, ngx * nx2 + 2, ngy * ny2 + 2 * PAD, LANES), f32),
            pltpu.VMEM((8, ngx * nx2, ngy * ny2, LANES), f32),
            pltpu.SemaphoreType.DMA((2, count)),
            pltpu.SemaphoreType.DMA((2, count)),
        ],
        compiler_params=pltpu.CompilerParams(
            collective_id=0, has_side_effects=True, vmem_limit_bytes=48 * 1024 * 1024
        ),
    )(source, labels, jitter, phase_sigma)


def solution(mesh):
    spec = P("gx", "gy", None)
    return jax.shard_map(
        functools.partial(per_device, mesh.shape["gx"], mesh.shape["gy"]),
        mesh=mesh, in_specs=(spec, spec, spec, P()), out_specs=(spec, spec, spec),
        check_vma=False,
    )
```

```python
import functools
import jax
import jax.numpy as jnp
from jax import lax
from jax.experimental import pallas as pl
from jax.experimental.pallas import tpu as pltpu
from jax.sharding import PartitionSpec as P

SWEEPS = 2
COARSE_SWEEPS = 8
PAD = 8
LANES = 128
STEPS = 5
MESH = pl.DeviceIdType.MESH


def pair_matrix(rows, columns):
    row = lax.broadcasted_iota(jnp.int32, (rows, columns), 0)
    column = lax.broadcasted_iota(jnp.int32, (rows, columns), 1)
    return jnp.where(lax.div(row, 2) == lax.rem(column, rows // 2), 0.125, 0.0).astype(jnp.float32)


def coarsen(values, tmp):
    extent_x, extent_y, extent_z = values.shape
    paired = values.reshape(extent_x // 2, 2, extent_y, extent_z)
    paired = (paired[:, 0] + paired[:, 1]).reshape(extent_x // 2 * extent_y, extent_z)
    paired = jnp.dot(
        paired, pair_matrix(extent_z, LANES), precision=lax.Precision.HIGHEST,
        preferred_element_type=jnp.float32,
    )
    rows = extent_x // 2 * extent_y
    tmp[pl.ds(0, rows), :] = paired
    summed = tmp[pl.ds(0, rows // 2, stride=2), :] + tmp[pl.ds(1, rows // 2, stride=2), :]
    return summed.reshape(extent_x // 2, extent_y // 2, LANES)


def iota(shape, dim):
    return lax.broadcasted_iota(jnp.int32, shape, dim)


def make_coeffs(out, rows, centre, others, edges, factor, source):
    face_weights = [
        jnp.where(edge, centre, 2.0 * centre * other / (centre + other))
        for other, edge in zip(others, edges)
    ]
    diagonal = face_weights[0]
    for weight in face_weights[1:]:
        diagonal = diagonal + weight
    inverse = 1.0 / diagonal
    for face in range(6):
        out[face, rows] = jnp.where(edges[face], 0.0, face_weights[face] * inverse)
    out[6, rows] = factor * inverse


def linked(coeffs, rows, others):
    summed = coeffs[0, rows] * others[0]
    for face in range(1, 6):
        summed = summed + coeffs[face, rows] * others[face]
    return summed


class Level:
    def __init__(self, ref, coeffs, halos, sems, counts, extent_z, factor):
        self.ref, self.coeffs = ref, coeffs
        self.xlo, self.xhi, self.ylo, self.yhi = halos
        self.send, self.recv = sems
        self.nx = ref.shape[1]
        self.ny = ref.shape[2] - 2 * PAD
        self.nz = ref.shape[3]
        self.factor = factor
        self.ngx, self.ngy = counts
        self.gx, self.gy = lax.axis_index("gx"), lax.axis_index("gy")

    def copies(self, step):
        kind = 0 if step == 0 else 1
        ref, ny = self.ref.at[kind], self.ny
        ends = [
            (ref.at[0, pl.ds(PAD, ny)], self.xhi, {"gx": self.gx - 1}),
            (ref.at[self.nx - 1, pl.ds(PAD, ny)], self.xlo, {"gx": self.gx + 1}),
            (ref.at[:, pl.ds(PAD, 8)], self.yhi, {"gy": self.gy - 1}),
            (ref.at[:, pl.ds(PAD + ny - 8, 8)], self.ylo, {"gy": self.gy + 1}),
        ]
        return [
            pltpu.make_async_remote_copy(
                src_ref=src, dst_ref=dst.at[step], send_sem=self.send.at[step, place],
                recv_sem=self.recv.at[step, place], device_id=device, device_id_type=MESH,
            )
            for place, (src, dst, device) in enumerate(ends)
        ]

    def sides(self):
        return [
            self.gx > 0, self.gx < self.ngx - 1, self.gy > 0, self.gy < self.ngy - 1,
        ]

    def clear(self):
        for there, buf in zip(self.sides(), (self.xlo, self.xhi, self.ylo, self.yhi)):
            @pl.when(jnp.logical_not(there))
            def _():
                buf[...] = jnp.zeros_like(buf)

    def start(self, step):
        copies = self.copies(step)
        for place in (2, 3, 0, 1):
            pl.when(self.sides()[place])(copies[place].start)

    def wait(self, step):
        copies = self.copies(step)
        opposite = (1, 0, 3, 2)
        for place in range(4):
            @pl.when(self.sides()[place])
            def _():
                copies[place].wait_send()
                copies[opposite[place]].wait_recv()
        kind = 0 if step == 0 else 1
        self.ref[kind, :, pl.ds(PAD - 1, 1), :] = self.ylo[step, :, 7:8, :]
        self.ref[kind, :, pl.ds(PAD + self.ny, 1), :] = self.yhi[step, :, 0:1, :]

    def others(self, step):
        kind = 0 if step == 0 else 1
        ref, ny, nz = self.ref.at[kind], self.ny, self.nz
        centre = ref[:, pl.ds(PAD, ny), :]
        above = jnp.concatenate([centre[1:], self.xhi[step][None]], axis=0)
        below = jnp.concatenate([self.xlo[step][None], centre[:-1]], axis=0)
        return centre, [
            above, below,
            ref[:, pl.ds(PAD + 1, ny), :], ref[:, pl.ds(PAD - 1, ny), :],
            pltpu.roll(centre, nz - 1, 2), pltpu.roll(centre, 1, 2),
        ]

    def weigh(self):
        centre, others = self.others(0)
        shape = centre.shape
        at_x, at_y, at_z = (iota(shape, dim) for dim in range(3))
        at_x, at_y = at_x + self.gx * self.nx, at_y + self.gy * self.ny
        edges = [
            at_x == self.ngx * self.nx - 1, at_x == 0, at_y == self.ngy * self.ny - 1, at_y == 0,
            at_z == self.nz - 1, at_z == 0,
        ]
        make_coeffs(self.coeffs, slice(None), centre, others, edges, self.factor, None)

    def colour(self):
        shape = (self.nx, self.ny, self.nz)
        total = iota(shape, 0) + iota(shape, 1) + iota(shape, 2)
        return lax.rem(total + self.gx * self.nx + self.gy * self.ny, 2) == 0

    def smooth(self, source, beside):
        rows = slice(None)
        coeffs, own = self.coeffs, (1, slice(None), pl.ds(PAD, self.ny))
        right = source * coeffs[6, rows]
        self.right[...] = right
        self.ref[own] = jnp.where(self.colour(), right, 0.0)
        for step in range(1, STEPS):
            self.start(step)
            if step - 1 < len(beside):
                beside[step - 1]()
            self.wait(step)
            centre, others = self.others(step)
            fresh = self.right[...] + linked(coeffs, rows, others)
            if step < STEPS - 1:
                red = self.colour()
                turn = red if step % 2 == 0 else jnp.logical_not(red)
                self.ref[own] = jnp.where(turn, fresh, centre)
            else:
                return (fresh - centre) / coeffs[6, rows]


class Deep:
    REACH = 2 * SWEEPS

    def __init__(self, cells, coeffs, sems, counts, shape, factor):
        self.cells, self.coeffs = cells, coeffs
        self.send, self.recv = sems
        self.nx, self.ny, self.nz = shape
        self.factor = factor
        self.ngx, self.ngy = counts
        self.gx, self.gy = lax.axis_index("gx"), lax.axis_index("gy")
        self.rim = (cells.shape[1] - self.nx) // 2
        self.rows = self.ny + 2 * PAD

    def own(self, kind):
        return self.cells.at[kind, pl.ds(self.rim, self.nx), pl.ds(PAD, self.ny)]

    def exchange(self, kind, starts):
        cells = self.cells.at[kind]
        far = -(-(self.REACH + 1 - kind) // self.nx)
        number = 0
        for dx in range(-far, far + 1):
            for dy in (0, -1, 1):
                if dx == 0 and dy == 0:
                    continue
                x, y = self.gx + dx, self.gy + dy
                back_x, back_y = self.gx - dx, self.gy - dy
                rows = self.ny if dy == 0 else PAD
                first = {0: PAD, -1: PAD, 1: self.ny}[dy]
                there = {0: PAD, -1: PAD + self.ny, 1: 0}[dy]
                copy = pltpu.make_async_remote_copy(
                    src_ref=cells.at[pl.ds(self.rim, self.nx), pl.ds(first, rows)],
                    dst_ref=cells.at[pl.ds(self.rim - dx * self.nx, self.nx), pl.ds(there, rows)],
                    send_sem=self.send.at[kind, number], recv_sem=self.recv.at[kind, number],
                    device_id=(x, y), device_id_type=MESH,
                )
                number += 1
                sends = inside(x, self.ngx, dx) & inside(y, self.ngy, dy)
                comes = inside(back_x, self.ngx, dx) & inside(back_y, self.ngy, dy)
                if starts:
                    pl.when(sends)(copy.start)
                else:
                    pl.when(sends)(copy.wait_send)
                    pl.when(comes)(copy.wait_recv)

    def span(self, reach):
        return pl.ds(self.rim - reach, self.nx + 2 * reach)

    def others(self, kind, reach):
        cells = self.cells.at[kind]
        centre = cells[self.span(reach)]
        low = self.rim - reach
        return centre, [
            cells[pl.ds(low + 1, self.nx + 2 * reach)], cells[pl.ds(low - 1, self.nx + 2 * reach)],
            pltpu.roll(centre, self.rows - 1, 1), pltpu.roll(centre, 1, 1),
            pltpu.roll(centre, self.nz - 1, 2), pltpu.roll(centre, 1, 2),
        ]

    def weigh(self):
        centre, others = self.others(0, self.REACH)
        at_x, at_y, at_z = (iota(centre.shape, dim) for dim in range(3))
        at_x = at_x + self.gx * self.nx - self.REACH
        at_y = at_y + self.gy * self.ny - PAD
        edges = [
            at_x == self.ngx * self.nx - 1, at_x == 0, at_y == self.ngy * self.ny - 1, at_y == 0,
            at_z == self.nz - 1, at_z == 0,
        ]
        make_coeffs(self.coeffs, slice(None), centre, others, edges, self.factor, None)

    def planes(self, reach):
        return pl.ds(self.REACH - reach, self.nx + 2 * reach)

    def red(self, reach):
        shape = (self.nx + 2 * reach, self.rows, self.nz)
        total = iota(shape, 0) + iota(shape, 1) + iota(shape, 2)
        start = self.gx * self.nx + self.gy * self.ny + 2 * self.REACH - reach
        return lax.rem(total + start, 2) == 0

    def smooth(self):
        reach = self.REACH
        right = self.cells[1, self.span(reach)] * self.coeffs[6]
        self.coeffs[7] = right
        self.cells[2, self.span(reach)] = jnp.where(self.red(reach), right, 0.0)
        for reach in range(self.REACH - 1, -1, -1):
            centre, others = self.others(2, reach)
            here = self.planes(reach)
            fresh = self.coeffs[7, here] + linked(self.coeffs, here, others)
            if reach:
                red = self.red(reach)
                turn = red if reach % 2 == 0 else jnp.logical_not(red)
                self.cells[2, self.span(reach)] = jnp.where(turn, fresh, centre)
        remainder = (fresh - centre) / self.coeffs[6, self.planes(0)]
        return remainder[:, PAD : PAD + self.ny]


def inside(index, count, shift):
    if shift == 0:
        return True
    return jnp.logical_and(index >= 0, index < count)


def kernel(ngx, ngy, src, lab, jit, phase, out0, out1, out2,
           f0, c0, r0, xl0, xh0, yl0, yh0, s0, v0,
           f1, c1, s1, v1, inputs, labels, loads,
           tmp, block, grid, c2, gsend, grecv):
    gx, gy = lax.axis_index("gx"), lax.axis_index("gy")
    me, count = gx * ngy + gy, ngx * ngy
    fine = Level(f0, c0, (xl0, xh0, yl0, yh0), (s0, v0), (ngx, ngy), src.shape[2], 1.0)
    half_shape = tuple(extent // 2 for extent in src.shape)
    mid = Deep(f1, c1, (s1, v1), (ngx, ngy), half_shape, 4.0)
    fine.right = r0
    fetches = [
        pltpu.make_async_copy(array, inputs.at[place], loads.at[place])
        for place, array in enumerate((jit, src))
    ]
    fetches.append(pltpu.make_async_copy(lab, labels, loads.at[2]))
    for fetch in fetches:
        fetch.start()
    nx2, ny2 = block.shape[1], block.shape[2]
    big_x, big_y = ngx * nx2, ngy * ny2
    deep = src.shape[2] // 4

    fine.clear()
    f1[0] = jnp.ones_like(f1.at[0])
    f1[1] = jnp.zeros_like(f1.at[1])
    grid[...] = jnp.zeros_like(grid)

    def target(offset):
        other = lax.rem(me + offset, count)
        return (lax.div(other, ngy), lax.rem(other, ngy))

    barrier = pltpu.get_barrier_semaphore()

    def greet(offset, carry):
        pl.semaphore_signal(barrier, inc=1, device_id=target(offset), device_id_type=MESH)
        return carry

    lax.fori_loop(1, count, greet, 0)

    fetches[0].wait()
    fetches[2].wait()
    sigma = jnp.where(labels[...] == 1, phase[1], phase[0]) * inputs[0]
    fine.ref[0, :, pl.ds(PAD, fine.ny), :] = sigma
    pl.semaphore_wait(barrier, count - 1)
    fine.start(0)

    def place(kind, x, y):
        return grid.at[kind, pl.ds(1 + x * nx2, nx2), pl.ds(pl.multiple_of(PAD + y * ny2, 8), ny2)]

    def gather_copy(kind, offset, sender):
        return pltpu.make_async_remote_copy(
            src_ref=block.at[kind], dst_ref=place(kind, gx, gy), send_sem=gsend.at[kind, offset],
            recv_sem=grecv.at[kind, sender], device_id=target(offset), device_id_type=MESH,
        )

    def gather_start(kind, values):
        block[kind] = values
        place(kind, gx, gy)[...] = values

        def push(offset, carry):
            gather_copy(kind, offset, me).start()
            return carry

        lax.fori_loop(1, count, push, 0)

    def gather_wait(kind):
        def pull(offset, carry):
            copy = gather_copy(kind, offset, lax.rem(me + offset, count))
            copy.wait_send()
            copy.wait_recv()
            return carry

        lax.fori_loop(1, count, pull, 0)

    sigma1 = coarsen(sigma, tmp)
    mid.own(0)[...] = sigma1
    mid.exchange(0, True)
    gather_start(0, coarsen(sigma1, tmp))
    fine.wait(0)
    fine.weigh()
    fetches[1].wait()

    def mid_weights():
        mid.exchange(0, False)
        mid.weigh()

    chunk = min(big_x, 16)
    rows_y = pl.ds(PAD, big_y)

    def chunks(body):
        if big_x == chunk:
            body(0)
        else:
            def step(index, carry):
                body(index * chunk)
                return carry
            lax.fori_loop(0, big_x // chunk, step, 0)

    def grid_others(kind, first):
        ref = grid.at[kind]
        here = pl.ds(1 + first, chunk)
        centre = ref[here, rows_y, :]
        return centre, [
            ref[pl.ds(2 + first, chunk), rows_y, :], ref[pl.ds(first, chunk), rows_y, :],
            ref[here, pl.ds(PAD + 1, big_y), :], ref[here, pl.ds(PAD - 1, big_y), :],
            pltpu.roll(centre, LANES - 1, 2), pltpu.roll(centre, 1, 2),
        ]

    def coarse_weights():
        gather_wait(0)

        def weigh(first):
            centre, others = grid_others(0, first)
            shape = centre.shape
            at_x, at_y, at_z = (iota(shape, dim) for dim in range(3))
            at_x = at_x + first
            edges = [
                at_x == big_x - 1, at_x == 0, at_y == big_y - 1, at_y == 0,
                lax.rem(at_z, deep) == deep - 1, lax.rem(at_z, deep) == 0,
            ]
            make_coeffs(c2, pl.ds(first, chunk), centre, others, edges, 16.0, None)

        chunks(weigh)

    remainder = fine.smooth(inputs[1], [mid_weights, coarse_weights])
    mid.own(1)[...] = coarsen(remainder, tmp)
    mid.exchange(1, True)
    out0[...] = f0[1, :, pl.ds(PAD, fine.ny), :]
    mid.exchange(1, False)
    gather_start(1, coarsen(mid.smooth(), tmp))
    out1[...] = mid.own(2)[...]
    gather_wait(1)

    def colour(first):
        shape = (chunk, big_y, LANES)
        return lax.rem(iota(shape, 0) + iota(shape, 1) + iota(shape, 2) + first, 2) == 0

    def first_red(first):
        here = pl.ds(first, chunk)
        right = grid[1, pl.ds(1 + first, chunk), rows_y, :] * c2[6, here]
        c2[7, here] = right
        grid[2, pl.ds(1 + first, chunk), rows_y, :] = jnp.where(colour(first), right, 0.0)

    def half(parity):
        def body(first):
            here = pl.ds(first, chunk)
            centre, others = grid_others(2, first)
            fresh = c2[7, here] + linked(c2, here, others)
            red = colour(first)
            turn = red if parity == 0 else jnp.logical_not(red)
            grid[2, pl.ds(1 + first, chunk), rows_y, :] = jnp.where(turn, fresh, centre)
        chunks(body)

    chunks(first_red)
    half(1)

    def sweep(repeat, carry):
        half(0)
        half(1)
        return carry

    lax.fori_loop(0, COARSE_SWEEPS - 1, sweep, 0)
    mine = place(2, gx, gy)[...]
    out2[...] = mine[:, :, :deep]


def per_device(ngx, ngy, source, labels, jitter, phase_sigma):
    nx, ny, nz = source.shape
    count = ngx * ngy
    f32 = jnp.float32

    def level(nx, ny, nz):
        return [
            pltpu.VMEM((2, nx, ny + 2 * PAD, nz), f32),
            pltpu.VMEM((7, nx, ny, nz), f32),
            pltpu.VMEM((nx, ny, nz), f32),
            pltpu.VMEM((STEPS, ny, nz), f32),
            pltpu.VMEM((STEPS, ny, nz), f32),
            pltpu.VMEM((STEPS, nx, 8, nz), f32),
            pltpu.VMEM((STEPS, nx, 8, nz), f32),
            pltpu.SemaphoreType.DMA((STEPS, 4)),
            pltpu.SemaphoreType.DMA((STEPS, 4)),
        ]

    def deep(nx, ny, nz):
        far = -(-(Deep.REACH + 1) // nx)
        return [
            pltpu.VMEM((3, nx + 2 * far * nx, ny + 2 * PAD, nz), f32),
            pltpu.VMEM((8, nx + 2 * Deep.REACH, ny + 2 * PAD, nz), f32),
            pltpu.SemaphoreType.DMA((2, 6 * far + 2)),
            pltpu.SemaphoreType.DMA((2, 6 * far + 2)),
        ]

    nx2, ny2 = nx // 4, ny // 4
    vmem = pl.BlockSpec(memory_space=pltpu.VMEM)
    hbm = pl.BlockSpec(memory_space=pl.ANY)
    return pl.pallas_call(
        functools.partial(kernel, ngx, ngy),
        out_shape=(
            jax.ShapeDtypeStruct((nx, ny, nz), f32),
            jax.ShapeDtypeStruct((nx // 2, ny // 2, nz // 2), f32),
            jax.ShapeDtypeStruct((nx2, ny2, nz // 4), f32),
        ),
        in_specs=[hbm, hbm, hbm, pl.BlockSpec(memory_space=pltpu.SMEM)],
        out_specs=(vmem, vmem, vmem),
        scratch_shapes=level(nx, ny, nz) + deep(nx // 2, ny // 2, nz // 2) + [
            pltpu.VMEM((2, nx, ny, nz), f32),
            pltpu.VMEM((nx, ny, nz), jnp.int32),
            pltpu.SemaphoreType.DMA((3,)),
            pltpu.VMEM((nx // 2 * ny, LANES), f32),
            pltpu.VMEM((2, nx2, ny2, LANES), f32),
            pltpu.VMEM((3, ngx * nx2 + 2, ngy * ny2 + 2 * PAD, LANES), f32),
            pltpu.VMEM((8, ngx * nx2, ngy * ny2, LANES), f32),
            pltpu.SemaphoreType.DMA((2, count)),
            pltpu.SemaphoreType.DMA((2, count)),
        ],
        compiler_params=pltpu.CompilerParams(
            collective_id=0, has_side_effects=True, vmem_limit_bytes=60 * 1024 * 1024
        ),
    )(source, labels, jitter, phase_sigma)


def solution(mesh):
    spec = P("gx", "gy", None)
    return jax.shard_map(
        functools.partial(per_device, mesh.shape["gx"], mesh.shape["gy"]),
        mesh=mesh, in_specs=(spec, spec, spec, P()), out_specs=(spec, spec, spec),
        check_vma=False,
    )
```

```python
import functools
import jax
import jax.numpy as jnp
from jax import lax
from jax.experimental import pallas as pl
from jax.experimental.pallas import tpu as pltpu
from jax.sharding import PartitionSpec as P

SWEEPS = 2
COARSE_SWEEPS = 8
PAD = 8
LANES = 128
MESH = pl.DeviceIdType.MESH


def pair_matrix(rows, columns):
    row = lax.broadcasted_iota(jnp.int32, (rows, columns), 0)
    column = lax.broadcasted_iota(jnp.int32, (rows, columns), 1)
    return jnp.where(lax.div(row, 2) == lax.rem(column, rows // 2), 0.125, 0.0).astype(jnp.float32)


def coarsen(values, tmp):
    extent_x, extent_y, extent_z = values.shape
    paired = values.reshape(extent_x // 2, 2, extent_y, extent_z)
    paired = (paired[:, 0] + paired[:, 1]).reshape(extent_x // 2 * extent_y, extent_z)
    paired = jnp.dot(
        paired, pair_matrix(extent_z, LANES), precision=lax.Precision.HIGHEST,
        preferred_element_type=jnp.float32,
    )
    rows = extent_x // 2 * extent_y
    tmp[pl.ds(0, rows), :] = paired
    summed = tmp[pl.ds(0, rows // 2, stride=2), :] + tmp[pl.ds(1, rows // 2, stride=2), :]
    return summed.reshape(extent_x // 2, extent_y // 2, LANES)


def iota(shape, dim):
    return lax.broadcasted_iota(jnp.int32, shape, dim)


def make_coeffs(out, rows, centre, others, edges, factor, source):
    face_weights = [
        jnp.where(edge, centre, 2.0 * centre * other / (centre + other))
        for other, edge in zip(others, edges)
    ]
    diagonal = face_weights[0]
    for weight in face_weights[1:]:
        diagonal = diagonal + weight
    inverse = 1.0 / diagonal
    for face in range(6):
        out[face, rows] = jnp.where(edges[face], 0.0, face_weights[face] * inverse)
    out[6, rows] = factor * inverse


def linked(coeffs, rows, others):
    summed = coeffs[0, rows] * others[0]
    for face in range(1, 6):
        summed = summed + coeffs[face, rows] * others[face]
    return summed


class Deep:
    REACH = 2 * SWEEPS

    def __init__(self, cells, coeffs, sems, counts, shape, factor):
        self.cells, self.coeffs = cells, coeffs
        self.send, self.recv = sems
        self.nx, self.ny, self.nz = shape
        self.factor = factor
        self.ngx, self.ngy = counts
        self.gx, self.gy = lax.axis_index("gx"), lax.axis_index("gy")
        self.rim = (cells.shape[1] - self.nx) // 2
        self.rows = self.ny + 2 * PAD

    def own(self, kind):
        return self.cells.at[kind, pl.ds(self.rim, self.nx), pl.ds(PAD, self.ny)]

    def exchange(self, kind, starts):
        cells = self.cells.at[kind]
        far = -(-(self.REACH + 1 - kind) // self.nx)
        number = 0
        for dx in range(-far, far + 1):
            for dy in (0, -1, 1):
                if dx == 0 and dy == 0:
                    continue
                x, y = self.gx + dx, self.gy + dy
                back_x, back_y = self.gx - dx, self.gy - dy
                rows = self.ny if dy == 0 else PAD
                first = {0: PAD, -1: PAD, 1: self.ny}[dy]
                there = {0: PAD, -1: PAD + self.ny, 1: 0}[dy]
                wide = self.nx
                if dx:
                    wide = min(wide, self.REACH + 1 - kind - (abs(dx) - 1) * self.nx)
                start = self.rim + (self.nx - wide if dx > 0 else 0)
                copy = pltpu.make_async_remote_copy(
                    src_ref=cells.at[pl.ds(start, wide), pl.ds(first, rows)],
                    dst_ref=cells.at[pl.ds(start - dx * self.nx, wide), pl.ds(there, rows)],
                    send_sem=self.send.at[kind, number], recv_sem=self.recv.at[kind, number],
                    device_id=(x, y), device_id_type=MESH,
                )
                number += 1
                sends = inside(x, self.ngx, dx) & inside(y, self.ngy, dy)
                comes = inside(back_x, self.ngx, dx) & inside(back_y, self.ngy, dy)
                if starts:
                    pl.when(sends)(copy.start)
                else:
                    pl.when(sends)(copy.wait_send)
                    pl.when(comes)(copy.wait_recv)

    def span(self, reach):
        return pl.ds(self.rim - reach, self.nx + 2 * reach)

    def others(self, kind, reach):
        cells = self.cells.at[kind]
        centre = cells[self.span(reach)]
        low = self.rim - reach
        return centre, [
            cells[pl.ds(low + 1, self.nx + 2 * reach)], cells[pl.ds(low - 1, self.nx + 2 * reach)],
            pltpu.roll(centre, self.rows - 1, 1), pltpu.roll(centre, 1, 1),
            pltpu.roll(centre, self.nz - 1, 2), pltpu.roll(centre, 1, 2),
        ]

    def weigh(self):
        centre, others = self.others(0, self.REACH)
        at_x, at_y, at_z = (iota(centre.shape, dim) for dim in range(3))
        at_x = at_x + self.gx * self.nx - self.REACH
        at_y = at_y + self.gy * self.ny - PAD
        edges = [
            at_x == self.ngx * self.nx - 1, at_x == 0, at_y == self.ngy * self.ny - 1, at_y == 0,
            at_z == self.nz - 1, at_z == 0,
        ]
        make_coeffs(self.coeffs, slice(None), centre, others, edges, self.factor, None)

    def planes(self, reach):
        return pl.ds(self.REACH - reach, self.nx + 2 * reach)

    def red(self, reach):
        shape = (self.nx + 2 * reach, self.rows, self.nz)
        total = iota(shape, 0) + iota(shape, 1) + iota(shape, 2)
        start = self.gx * self.nx + self.gy * self.ny + 2 * self.REACH - reach
        return lax.rem(total + start, 2) == 0

    def smooth(self):
        reach = self.REACH
        right = self.cells[1, self.span(reach)] * self.coeffs[6]
        self.coeffs[7] = right
        self.cells[2, self.span(reach)] = jnp.where(self.red(reach), right, 0.0)
        for reach in range(self.REACH - 1, -1, -1):
            centre, others = self.others(2, reach)
            here = self.planes(reach)
            fresh = self.coeffs[7, here] + linked(self.coeffs, here, others)
            if reach:
                red = self.red(reach)
                turn = red if reach % 2 == 0 else jnp.logical_not(red)
                self.cells[2, self.span(reach)] = jnp.where(turn, fresh, centre)
        remainder = (fresh - centre) / self.coeffs[6, self.planes(0)]
        return remainder[:, PAD : PAD + self.ny]


def inside(index, count, shift):
    if shift == 0:
        return True
    return jnp.logical_and(index >= 0, index < count)


def kernel(ngx, ngy, src, lab, jit, phase, out0, out1, out2,
           f0, c0, s0, v0,
           f1, c1, s1, v1, inputs, labels, held, loads,
           tmp, block, grid, c2, gsend, grecv):
    gx, gy = lax.axis_index("gx"), lax.axis_index("gy")
    me, count = gx * ngy + gy, ngx * ngy
    fine = Deep(f0, c0, (s0, v0), (ngx, ngy), src.shape, 1.0)
    half_shape = tuple(extent // 2 for extent in src.shape)
    mid = Deep(f1, c1, (s1, v1), (ngx, ngy), half_shape, 4.0)
    fetches = [
        pltpu.make_async_copy(jit, inputs, loads.at[0]),
        pltpu.make_async_copy(lab, labels, loads.at[1]),
        pltpu.make_async_copy(src, held, loads.at[2]),
    ]
    for fetch in fetches:
        fetch.start()
    nx2, ny2 = block.shape[1], block.shape[2]
    big_x, big_y = ngx * nx2, ngy * ny2
    deep = src.shape[2] // 4

    f0[0] = jnp.ones_like(f0.at[0])
    f0[1] = jnp.zeros_like(f0.at[1])
    f1[0] = jnp.ones_like(f1.at[0])
    f1[1] = jnp.zeros_like(f1.at[1])
    grid[...] = jnp.zeros_like(grid)

    def target(offset):
        other = lax.rem(me + offset, count)
        return (lax.div(other, ngy), lax.rem(other, ngy))

    barrier = pltpu.get_barrier_semaphore()

    def greet(offset, carry):
        pl.semaphore_signal(barrier, inc=1, device_id=target(offset), device_id_type=MESH)
        return carry

    lax.fori_loop(1, count, greet, 0)

    fetches[0].wait()
    fetches[1].wait()
    sigma = jnp.where(labels[...] == 1, phase[1], phase[0]) * inputs[...]
    fine.own(0)[...] = sigma
    fetches[2].wait()
    fine.own(1)[...] = held[...]
    pl.semaphore_wait(barrier, count - 1)
    fine.exchange(0, True)
    fine.exchange(1, True)

    def place(kind, x, y):
        return grid.at[kind, pl.ds(1 + x * nx2, nx2), pl.ds(pl.multiple_of(PAD + y * ny2, 8), ny2)]

    def gather_copy(kind, offset, sender):
        return pltpu.make_async_remote_copy(
            src_ref=block.at[kind], dst_ref=place(kind, gx, gy), send_sem=gsend.at[kind, offset],
            recv_sem=grecv.at[kind, sender], device_id=target(offset), device_id_type=MESH,
        )

    def gather_start(kind, values):
        block[kind] = values
        place(kind, gx, gy)[...] = values

        def push(offset, carry):
            gather_copy(kind, offset, me).start()
            return carry

        lax.fori_loop(1, count, push, 0)

    def gather_wait(kind):
        def pull(offset, carry):
            copy = gather_copy(kind, offset, lax.rem(me + offset, count))
            copy.wait_send()
            copy.wait_recv()
            return carry

        lax.fori_loop(1, count, pull, 0)

    sigma1 = coarsen(sigma, tmp)
    mid.own(0)[...] = sigma1
    mid.exchange(0, True)
    gather_start(0, coarsen(sigma1, tmp))
    fine.exchange(0, False)
    fine.weigh()
    fine.exchange(1, False)

    def mid_weights():
        mid.exchange(0, False)
        mid.weigh()

    chunk = min(big_x, 16)
    rows_y = pl.ds(PAD, big_y)

    def chunks(body):
        if big_x == chunk:
            body(0)
        else:
            def step(index, carry):
                body(index * chunk)
                return carry
            lax.fori_loop(0, big_x // chunk, step, 0)

    def grid_others(kind, first):
        ref = grid.at[kind]
        here = pl.ds(1 + first, chunk)
        centre = ref[here, rows_y, :]
        return centre, [
            ref[pl.ds(2 + first, chunk), rows_y, :], ref[pl.ds(first, chunk), rows_y, :],
            ref[here, pl.ds(PAD + 1, big_y), :], ref[here, pl.ds(PAD - 1, big_y), :],
            pltpu.roll(centre, LANES - 1, 2), pltpu.roll(centre, 1, 2),
        ]

    def coarse_weights():
        gather_wait(0)

        def weigh(first):
            centre, others = grid_others(0, first)
            shape = centre.shape
            at_x, at_y, at_z = (iota(shape, dim) for dim in range(3))
            at_x = at_x + first
            edges = [
                at_x == big_x - 1, at_x == 0, at_y == big_y - 1, at_y == 0,
                lax.rem(at_z, deep) == deep - 1, lax.rem(at_z, deep) == 0,
            ]
            make_coeffs(c2, pl.ds(first, chunk), centre, others, edges, 16.0, None)

        chunks(weigh)

    mid.own(1)[...] = coarsen(fine.smooth(), tmp)
    mid.exchange(1, True)
    out0[...] = fine.own(2)[...]
    mid_weights()
    mid.exchange(1, False)
    gather_start(1, coarsen(mid.smooth(), tmp))
    out1[...] = mid.own(2)[...]
    coarse_weights()
    gather_wait(1)

    def colour(first):
        shape = (chunk, big_y, LANES)
        return lax.rem(iota(shape, 0) + iota(shape, 1) + iota(shape, 2) + first, 2) == 0

    def first_red(first):
        here = pl.ds(first, chunk)
        right = grid[1, pl.ds(1 + first, chunk), rows_y, :] * c2[6, here]
        c2[7, here] = right
        grid[2, pl.ds(1 + first, chunk), rows_y, :] = jnp.where(colour(first), right, 0.0)

    def half(parity):
        def body(first):
            here = pl.ds(first, chunk)
            centre, others = grid_others(2, first)
            fresh = c2[7, here] + linked(c2, here, others)
            red = colour(first)
            turn = red if parity == 0 else jnp.logical_not(red)
            grid[2, pl.ds(1 + first, chunk), rows_y, :] = jnp.where(turn, fresh, centre)
        chunks(body)

    chunks(first_red)
    half(1)

    def sweep(repeat, carry):
        half(0)
        half(1)
        return carry

    lax.fori_loop(0, COARSE_SWEEPS - 1, sweep, 0)
    mine = place(2, gx, gy)[...]
    out2[...] = mine[:, :, :deep]


def per_device(ngx, ngy, source, labels, jitter, phase_sigma):
    nx, ny, nz = source.shape
    count = ngx * ngy
    f32 = jnp.float32

    def deep(nx, ny, nz):
        far = -(-(Deep.REACH + 1) // nx)
        return [
            pltpu.VMEM((3, nx + 2 * far * nx, ny + 2 * PAD, nz), f32),
            pltpu.VMEM((8, nx + 2 * Deep.REACH, ny + 2 * PAD, nz), f32),
            pltpu.SemaphoreType.DMA((2, 6 * far + 2)),
            pltpu.SemaphoreType.DMA((2, 6 * far + 2)),
        ]

    nx2, ny2 = nx // 4, ny // 4
    vmem = pl.BlockSpec(memory_space=pltpu.VMEM)
    hbm = pl.BlockSpec(memory_space=pl.ANY)
    return pl.pallas_call(
        functools.partial(kernel, ngx, ngy),
        out_shape=(
            jax.ShapeDtypeStruct((nx, ny, nz), f32),
            jax.ShapeDtypeStruct((nx // 2, ny // 2, nz // 2), f32),
            jax.ShapeDtypeStruct((nx2, ny2, nz // 4), f32),
        ),
        in_specs=[hbm, hbm, hbm, pl.BlockSpec(memory_space=pltpu.SMEM)],
        out_specs=(vmem, vmem, vmem),
        scratch_shapes=deep(nx, ny, nz) + deep(nx // 2, ny // 2, nz // 2) + [
            pltpu.VMEM((nx, ny, nz), f32),
            pltpu.VMEM((nx, ny, nz), jnp.int32),
            pltpu.VMEM((nx, ny, nz), f32),
            pltpu.SemaphoreType.DMA((3,)),
            pltpu.VMEM((nx // 2 * ny, LANES), f32),
            pltpu.VMEM((2, nx2, ny2, LANES), f32),
            pltpu.VMEM((3, ngx * nx2 + 2, ngy * ny2 + 2 * PAD, LANES), f32),
            pltpu.VMEM((8, ngx * nx2, ngy * ny2, LANES), f32),
            pltpu.SemaphoreType.DMA((2, count)),
            pltpu.SemaphoreType.DMA((2, count)),
        ],
        compiler_params=pltpu.CompilerParams(
            collective_id=0, has_side_effects=True, vmem_limit_bytes=60 * 1024 * 1024
        ),
    )(source, labels, jitter, phase_sigma)


def solution(mesh):
    spec = P("gx", "gy", None)
    return jax.shard_map(
        functools.partial(per_device, mesh.shape["gx"], mesh.shape["gy"]),
        mesh=mesh, in_specs=(spec, spec, spec, P()), out_specs=(spec, spec, spec),
        check_vma=False,
    )
```

```python
import functools
import jax
import jax.numpy as jnp
from jax import lax
from jax.experimental import pallas as pl
from jax.experimental.pallas import tpu as pltpu
from jax.sharding import PartitionSpec as P

SWEEPS = 2
COARSE_SWEEPS = 8
PAD = 8
LANES = 128
MESH = pl.DeviceIdType.MESH


def pair_matrix(rows, columns):
    row = lax.broadcasted_iota(jnp.int32, (rows, columns), 0)
    column = lax.broadcasted_iota(jnp.int32, (rows, columns), 1)
    return jnp.where(lax.div(row, 2) == lax.rem(column, rows // 2), 0.125, 0.0).astype(jnp.float32)


def coarsen(values, tmp):
    extent_x, extent_y, extent_z = values.shape
    paired = values.reshape(extent_x // 2, 2, extent_y, extent_z)
    paired = (paired[:, 0] + paired[:, 1]).reshape(extent_x // 2 * extent_y, extent_z)
    paired = jnp.dot(
        paired, pair_matrix(extent_z, LANES), precision=lax.Precision.HIGHEST,
        preferred_element_type=jnp.float32,
    )
    rows = extent_x // 2 * extent_y
    tmp[pl.ds(0, rows), :] = paired
    summed = tmp[pl.ds(0, rows // 2, stride=2), :] + tmp[pl.ds(1, rows // 2, stride=2), :]
    return summed.reshape(extent_x // 2, extent_y // 2, LANES)


def iota(shape, dim):
    return lax.broadcasted_iota(jnp.int32, shape, dim)


def make_coeffs(out, rows, centre, others, edges, factor, source):
    face_weights = [
        jnp.where(edge, centre, 2.0 * centre * other / (centre + other))
        for other, edge in zip(others, edges)
    ]
    diagonal = face_weights[0]
    for weight in face_weights[1:]:
        diagonal = diagonal + weight
    inverse = 1.0 / diagonal
    for face in range(6):
        out[face, rows] = jnp.where(edges[face], 0.0, face_weights[face] * inverse)
    out[6, rows] = factor * inverse


def linked(coeffs, rows, others):
    summed = coeffs[0, rows] * others[0]
    for face in range(1, 6):
        summed = summed + coeffs[face, rows] * others[face]
    return summed


class Deep:
    REACH = 2 * SWEEPS

    def __init__(self, cells, coeffs, sems, counts, shape, factor):
        self.cells, self.coeffs = cells, coeffs
        self.send, self.recv = sems
        self.nx, self.ny, self.nz = shape
        self.factor = factor
        self.ngx, self.ngy = counts
        self.gx, self.gy = lax.axis_index("gx"), lax.axis_index("gy")
        self.rim = (cells.shape[1] - self.nx) // 2
        self.rows = self.ny + 2 * PAD

    def own(self, kind):
        return self.cells.at[kind, pl.ds(self.rim, self.nx), pl.ds(PAD, self.ny)]

    def exchange(self, kind, starts):
        cells = self.cells.at[kind]
        far = -(-(self.REACH + 1 - kind) // self.nx)
        number = 0
        for dx in range(-far, far + 1):
            for dy in (0, -1, 1):
                if dx == 0 and dy == 0:
                    continue
                x, y = self.gx + dx, self.gy + dy
                back_x, back_y = self.gx - dx, self.gy - dy
                rows = self.ny if dy == 0 else PAD
                first = {0: PAD, -1: PAD, 1: self.ny}[dy]
                there = {0: PAD, -1: PAD + self.ny, 1: 0}[dy]
                wide = self.nx
                if dx:
                    wide = min(wide, self.REACH + 1 - kind - (abs(dx) - 1) * self.nx)
                start = self.rim + (self.nx - wide if dx > 0 else 0)
                copy = pltpu.make_async_remote_copy(
                    src_ref=cells.at[pl.ds(start, wide), pl.ds(first, rows)],
                    dst_ref=cells.at[pl.ds(start - dx * self.nx, wide), pl.ds(there, rows)],
                    send_sem=self.send.at[kind, number], recv_sem=self.recv.at[kind, number],
                    device_id=(x, y), device_id_type=MESH,
                )
                number += 1
                sends = inside(x, self.ngx, dx) & inside(y, self.ngy, dy)
                comes = inside(back_x, self.ngx, dx) & inside(back_y, self.ngy, dy)
                if starts:
                    pl.when(sends)(copy.start)
                else:
                    pl.when(sends)(copy.wait_send)
                    pl.when(comes)(copy.wait_recv)

    def span(self, reach):
        return pl.ds(self.rim - reach, self.nx + 2 * reach)

    def others(self, kind, reach):
        cells = self.cells.at[kind]
        centre = cells[self.span(reach)]
        low = self.rim - reach
        return centre, [
            cells[pl.ds(low + 1, self.nx + 2 * reach)], cells[pl.ds(low - 1, self.nx + 2 * reach)],
            pltpu.roll(centre, self.rows - 1, 1), pltpu.roll(centre, 1, 1),
            pltpu.roll(centre, self.nz - 1, 2), pltpu.roll(centre, 1, 2),
        ]

    def weigh(self):
        centre, others = self.others(0, self.REACH)
        at_x, at_y, at_z = (iota(centre.shape, dim) for dim in range(3))
        at_x = at_x + self.gx * self.nx - self.REACH
        at_y = at_y + self.gy * self.ny - PAD
        edges = [
            at_x == self.ngx * self.nx - 1, at_x == 0, at_y == self.ngy * self.ny - 1, at_y == 0,
            at_z == self.nz - 1, at_z == 0,
        ]
        make_coeffs(self.coeffs, slice(None), centre, others, edges, self.factor, None)

    def planes(self, reach):
        return pl.ds(self.REACH - reach, self.nx + 2 * reach)

    def red(self, reach):
        shape = (self.nx + 2 * reach, self.rows, self.nz)
        total = iota(shape, 0) + iota(shape, 1) + iota(shape, 2)
        start = self.gx * self.nx + self.gy * self.ny + 2 * self.REACH - reach
        return lax.rem(total + start, 2) == 0

    def smooth(self):
        reach = self.REACH
        right = self.cells[1, self.span(reach)] * self.coeffs[6]
        self.coeffs[7] = right
        self.cells[2, self.span(reach)] = jnp.where(self.red(reach), right, 0.0)
        for reach in range(self.REACH - 1, -1, -1):
            centre, others = self.others(2, reach)
            here = self.planes(reach)
            fresh = self.coeffs[7, here] + linked(self.coeffs, here, others)
            if reach:
                red = self.red(reach)
                turn = red if reach % 2 == 0 else jnp.logical_not(red)
                self.cells[2, self.span(reach)] = jnp.where(turn, fresh, centre)
        remainder = (fresh - centre) / self.coeffs[6, self.planes(0)]
        return remainder[:, PAD : PAD + self.ny]


def inside(index, count, shift):
    if shift == 0:
        return True
    return jnp.logical_and(index >= 0, index < count)


def kernel(ngx, ngy, src, lab, jit, phase, out0, out1, out2,
           f0, c0, s0, v0,
           f1, c1, s1, v1, inputs, labels, held, loads,
           tmp, block, whole, grid, c2, gsend, grecv):
    gx, gy = lax.axis_index("gx"), lax.axis_index("gy")
    me, count = gx * ngy + gy, ngx * ngy
    fine = Deep(f0, c0, (s0, v0), (ngx, ngy), src.shape, 1.0)
    half_shape = tuple(extent // 2 for extent in src.shape)
    mid = Deep(f1, c1, (s1, v1), (ngx, ngy), half_shape, 4.0)
    fetches = [
        pltpu.make_async_copy(jit, inputs, loads.at[0]),
        pltpu.make_async_copy(lab, labels, loads.at[1]),
        pltpu.make_async_copy(src, held, loads.at[2]),
    ]
    for fetch in fetches:
        fetch.start()
    nx2, ny2 = block.shape[1], block.shape[2]
    big_x, big_y = ngx * nx2, ngy * ny2
    deep = src.shape[2] // 4

    f0[0] = jnp.ones_like(f0.at[0])
    f0[1] = jnp.zeros_like(f0.at[1])
    f1[0] = jnp.ones_like(f1.at[0])
    f1[1] = jnp.zeros_like(f1.at[1])
    grid[...] = jnp.zeros_like(grid)

    def target(offset):
        other = lax.rem(me + offset, count)
        return (lax.div(other, ngy), lax.rem(other, ngy))

    barrier = pltpu.get_barrier_semaphore()

    def greet(offset, carry):
        pl.semaphore_signal(barrier, inc=1, device_id=target(offset), device_id_type=MESH)
        return carry

    lax.fori_loop(1, count, greet, 0)

    fetches[0].wait()
    fetches[1].wait()
    sigma = jnp.where(labels[...] == 1, phase[1], phase[0]) * inputs[...]
    fine.own(0)[...] = sigma
    fetches[2].wait()
    fine.own(1)[...] = held[...]
    pl.semaphore_wait(barrier, count - 1)
    fine.exchange(0, True)
    fine.exchange(1, True)

    def place(kind, x, y):
        return grid.at[kind, pl.ds(1 + x * nx2, nx2), pl.ds(pl.multiple_of(PAD + y * ny2, 8), ny2)]

    def gather_copy(kind, offset, sender):
        return pltpu.make_async_remote_copy(
            src_ref=block.at[kind], dst_ref=place(kind, gx, gy), send_sem=gsend.at[kind],
            recv_sem=grecv.at[kind], device_id=target(offset), device_id_type=MESH,
        )

    def gather_start(kind, values):
        block[kind] = values
        place(kind, gx, gy)[...] = values

        def push(offset, carry):
            gather_copy(kind, offset, me).start()
            return carry

        lax.fori_loop(1, count, push, 0)

    def gather_wait(kind):
        pltpu.make_async_copy(whole, whole, gsend.at[kind]).wait()
        pltpu.make_async_copy(whole, whole, grecv.at[kind]).wait()

    sigma1 = coarsen(sigma, tmp)
    mid.own(0)[...] = sigma1
    mid.exchange(0, True)
    gather_start(0, coarsen(sigma1, tmp))
    fine.exchange(0, False)
    fine.weigh()
    fine.exchange(1, False)

    def mid_weights():
        mid.exchange(0, False)
        mid.weigh()

    chunk = min(big_x, 16)
    rows_y = pl.ds(PAD, big_y)

    def chunks(body):
        if big_x == chunk:
            body(0)
        else:
            def step(index, carry):
                body(index * chunk)
                return carry
            lax.fori_loop(0, big_x // chunk, step, 0)

    def grid_others(kind, first):
        ref = grid.at[kind]
        here = pl.ds(1 + first, chunk)
        centre = ref[here, rows_y, :]
        return centre, [
            ref[pl.ds(2 + first, chunk), rows_y, :], ref[pl.ds(first, chunk), rows_y, :],
            ref[here, pl.ds(PAD + 1, big_y), :], ref[here, pl.ds(PAD - 1, big_y), :],
            pltpu.roll(centre, LANES - 1, 2), pltpu.roll(centre, 1, 2),
        ]

    def coarse_weights():
        gather_wait(0)

        def weigh(first):
            centre, others = grid_others(0, first)
            shape = centre.shape
            at_x, at_y, at_z = (iota(shape, dim) for dim in range(3))
            at_x = at_x + first
            edges = [
                at_x == big_x - 1, at_x == 0, at_y == big_y - 1, at_y == 0,
                lax.rem(at_z, deep) == deep - 1, lax.rem(at_z, deep) == 0,
            ]
            make_coeffs(c2, pl.ds(first, chunk), centre, others, edges, 16.0, None)

        chunks(weigh)

    mid.own(1)[...] = coarsen(fine.smooth(), tmp)
    mid.exchange(1, True)
    out0[...] = fine.own(2)[...]
    mid_weights()
    mid.exchange(1, False)
    gather_start(1, coarsen(mid.smooth(), tmp))
    out1[...] = mid.own(2)[...]
    coarse_weights()
    gather_wait(1)

    def colour(first):
        shape = (chunk, big_y, LANES)
        return lax.rem(iota(shape, 0) + iota(shape, 1) + iota(shape, 2) + first, 2) == 0

    def first_red(first):
        here = pl.ds(first, chunk)
        right = grid[1, pl.ds(1 + first, chunk), rows_y, :] * c2[6, here]
        c2[7, here] = right
        grid[2, pl.ds(1 + first, chunk), rows_y, :] = jnp.where(colour(first), right, 0.0)

    def half(parity):
        def body(first):
            here = pl.ds(first, chunk)
            centre, others = grid_others(2, first)
            fresh = c2[7, here] + linked(c2, here, others)
            red = colour(first)
            turn = red if parity == 0 else jnp.logical_not(red)
            grid[2, pl.ds(1 + first, chunk), rows_y, :] = jnp.where(turn, fresh, centre)
        chunks(body)

    chunks(first_red)
    half(1)

    def sweep(repeat, carry):
        half(0)
        half(1)
        return carry

    lax.fori_loop(0, COARSE_SWEEPS - 1, sweep, 0)
    mine = place(2, gx, gy)[...]
    out2[...] = mine[:, :, :deep]


def per_device(ngx, ngy, source, labels, jitter, phase_sigma):
    nx, ny, nz = source.shape
    count = ngx * ngy
    f32 = jnp.float32

    def deep(nx, ny, nz):
        far = -(-(Deep.REACH + 1) // nx)
        return [
            pltpu.VMEM((3, nx + 2 * far * nx, ny + 2 * PAD, nz), f32),
            pltpu.VMEM((8, nx + 2 * Deep.REACH, ny + 2 * PAD, nz), f32),
            pltpu.SemaphoreType.DMA((2, 6 * far + 2)),
            pltpu.SemaphoreType.DMA((2, 6 * far + 2)),
        ]

    nx2, ny2 = nx // 4, ny // 4
    vmem = pl.BlockSpec(memory_space=pltpu.VMEM)
    hbm = pl.BlockSpec(memory_space=pl.ANY)
    return pl.pallas_call(
        functools.partial(kernel, ngx, ngy),
        out_shape=(
            jax.ShapeDtypeStruct((nx, ny, nz), f32),
            jax.ShapeDtypeStruct((nx // 2, ny // 2, nz // 2), f32),
            jax.ShapeDtypeStruct((nx2, ny2, nz // 4), f32),
        ),
        in_specs=[hbm, hbm, hbm, pl.BlockSpec(memory_space=pltpu.SMEM)],
        out_specs=(vmem, vmem, vmem),
        scratch_shapes=deep(nx, ny, nz) + deep(nx // 2, ny // 2, nz // 2) + [
            pltpu.VMEM((nx, ny, nz), f32),
            pltpu.VMEM((nx, ny, nz), jnp.int32),
            pltpu.VMEM((nx, ny, nz), f32),
            pltpu.SemaphoreType.DMA((3,)),
            pltpu.VMEM((nx // 2 * ny, LANES), f32),
            pltpu.VMEM((2, nx2, ny2, LANES), f32),
            pltpu.VMEM((count - 1, nx2, ny2, LANES), f32),
            pltpu.VMEM((3, ngx * nx2 + 2, ngy * ny2 + 2 * PAD, LANES), f32),
            pltpu.VMEM((8, ngx * nx2, ngy * ny2, LANES), f32),
            pltpu.SemaphoreType.DMA((2,)),
            pltpu.SemaphoreType.DMA((2,)),
        ],
        compiler_params=pltpu.CompilerParams(
            collective_id=0, has_side_effects=True, vmem_limit_bytes=60 * 1024 * 1024
        ),
    )(source, labels, jitter, phase_sigma)


def solution(mesh):
    spec = P("gx", "gy", None)
    return jax.shard_map(
        functools.partial(per_device, mesh.shape["gx"], mesh.shape["gy"]),
        mesh=mesh, in_specs=(spec, spec, spec, P()), out_specs=(spec, spec, spec),
        check_vma=False,
    )
```

```python
import functools
import jax
import jax.numpy as jnp
from jax import lax
from jax.experimental import pallas as pl
from jax.experimental.pallas import tpu as pltpu
from jax.sharding import PartitionSpec as P

SWEEPS = 2
COARSE_SWEEPS = 8
PAD = 8
LANES = 128
MESH = pl.DeviceIdType.MESH


def pair_matrix(rows, columns):
    row = lax.broadcasted_iota(jnp.int32, (rows, columns), 0)
    column = lax.broadcasted_iota(jnp.int32, (rows, columns), 1)
    return jnp.where(lax.div(row, 2) == lax.rem(column, rows // 2), 0.125, 0.0).astype(jnp.float32)


def coarsen(values, tmp):
    extent_x, extent_y, extent_z = values.shape
    paired = values.reshape(extent_x // 2, 2, extent_y, extent_z)
    paired = (paired[:, 0] + paired[:, 1]).reshape(extent_x // 2 * extent_y, extent_z)
    paired = jnp.dot(
        paired, pair_matrix(extent_z, LANES), precision=lax.Precision.HIGHEST,
        preferred_element_type=jnp.float32,
    )
    rows = extent_x // 2 * extent_y
    tmp[pl.ds(0, rows), :] = paired
    summed = tmp[pl.ds(0, rows // 2, stride=2), :] + tmp[pl.ds(1, rows // 2, stride=2), :]
    return summed.reshape(extent_x // 2, extent_y // 2, LANES)


def iota(shape, dim):
    return lax.broadcasted_iota(jnp.int32, shape, dim)


def make_coeffs(out, rows, centre, others, edges, factor, source):
    face_weights = [
        jnp.where(edge, centre, 2.0 * centre * other / (centre + other))
        for other, edge in zip(others, edges)
    ]
    diagonal = face_weights[0]
    for weight in face_weights[1:]:
        diagonal = diagonal + weight
    inverse = 1.0 / diagonal
    for face in range(6):
        out[face, rows] = jnp.where(edges[face], 0.0, face_weights[face] * inverse)
    out[6, rows] = factor * inverse


def linked(coeffs, rows, others):
    summed = coeffs[0, rows] * others[0]
    for face in range(1, 6):
        summed = summed + coeffs[face, rows] * others[face]
    return summed


class Deep:
    REACH = 2 * SWEEPS

    def __init__(self, cells, coeffs, sems, counts, shape, factor):
        self.cells, self.coeffs = cells, coeffs
        self.send, self.recv = sems
        self.nx, self.ny, self.nz = shape
        self.factor = factor
        self.ngx, self.ngy = counts
        self.gx, self.gy = lax.axis_index("gx"), lax.axis_index("gy")
        self.rim = (cells.shape[1] - self.nx) // 2
        self.rows = self.ny + 2 * PAD

    def own(self, kind):
        return self.cells.at[kind, pl.ds(self.rim, self.nx), pl.ds(PAD, self.ny)]

    def exchange(self, kind, starts):
        cells = self.cells.at[kind]
        far = -(-(self.REACH + 1 - kind) // self.nx)
        number = 0
        for dx in sorted(range(-far, far + 1), key=abs):
            for dy in (0, -1, 1):
                if dx == 0 and dy == 0:
                    continue
                x, y = self.gx + dx, self.gy + dy
                back_x, back_y = self.gx - dx, self.gy - dy
                rows = self.ny if dy == 0 else PAD
                first = {0: PAD, -1: PAD, 1: self.ny}[dy]
                there = {0: PAD, -1: PAD + self.ny, 1: 0}[dy]
                wide = self.nx
                if dx:
                    wide = min(wide, self.REACH + 1 - kind - (abs(dx) - 1) * self.nx)
                start = self.rim + (self.nx - wide if dx > 0 else 0)
                copy = pltpu.make_async_remote_copy(
                    src_ref=cells.at[pl.ds(start, wide), pl.ds(first, rows)],
                    dst_ref=cells.at[pl.ds(start - dx * self.nx, wide), pl.ds(there, rows)],
                    send_sem=self.send.at[kind, number], recv_sem=self.recv.at[kind, number],
                    device_id=(x, y), device_id_type=MESH,
                )
                number += 1
                sends = inside(x, self.ngx, dx) & inside(y, self.ngy, dy)
                comes = inside(back_x, self.ngx, dx) & inside(back_y, self.ngy, dy)
                if starts:
                    pl.when(sends)(copy.start)
                else:
                    pl.when(sends)(copy.wait_send)
                    pl.when(comes)(copy.wait_recv)

    def span(self, reach):
        return pl.ds(self.rim - reach, self.nx + 2 * reach)

    def others(self, kind, reach):
        cells = self.cells.at[kind]
        centre = cells[self.span(reach)]
        low = self.rim - reach
        return centre, [
            cells[pl.ds(low + 1, self.nx + 2 * reach)], cells[pl.ds(low - 1, self.nx + 2 * reach)],
            pltpu.roll(centre, self.rows - 1, 1), pltpu.roll(centre, 1, 1),
            pltpu.roll(centre, self.nz - 1, 2), pltpu.roll(centre, 1, 2),
        ]

    def weigh(self):
        centre, others = self.others(0, self.REACH)
        at_x, at_y, at_z = (iota(centre.shape, dim) for dim in range(3))
        at_x = at_x + self.gx * self.nx - self.REACH
        at_y = at_y + self.gy * self.ny - PAD
        edges = [
            at_x == self.ngx * self.nx - 1, at_x == 0, at_y == self.ngy * self.ny - 1, at_y == 0,
            at_z == self.nz - 1, at_z == 0,
        ]
        make_coeffs(self.coeffs, slice(None), centre, others, edges, self.factor, None)

    def planes(self, reach):
        return pl.ds(self.REACH - reach, self.nx + 2 * reach)

    def red(self, reach):
        shape = (self.nx + 2 * reach, self.rows, self.nz)
        total = iota(shape, 0) + iota(shape, 1) + iota(shape, 2)
        start = self.gx * self.nx + self.gy * self.ny + 2 * self.REACH - reach
        return lax.rem(total + start, 2) == 0

    def smooth(self):
        reach = self.REACH
        right = self.cells[1, self.span(reach)] * self.coeffs[6]
        self.coeffs[7] = right
        self.cells[2, self.span(reach)] = jnp.where(self.red(reach), right, 0.0)
        for reach in range(self.REACH - 1, -1, -1):
            centre, others = self.others(2, reach)
            here = self.planes(reach)
            fresh = self.coeffs[7, here] + linked(self.coeffs, here, others)
            if reach:
                red = self.red(reach)
                turn = red if reach % 2 == 0 else jnp.logical_not(red)
                self.cells[2, self.span(reach)] = jnp.where(turn, fresh, centre)
        remainder = (fresh - centre) / self.coeffs[6, self.planes(0)]
        return remainder[:, PAD : PAD + self.ny]


def inside(index, count, shift):
    if shift == 0:
        return True
    return jnp.logical_and(index >= 0, index < count)


def kernel(ngx, ngy, src, lab, jit, phase, out0, out1, out2,
           f0, c0, s0, v0,
           f1, c1, s1, v1, inputs, labels, held, loads,
           tmp, block, whole, grid, c2, gsend, grecv):
    gx, gy = lax.axis_index("gx"), lax.axis_index("gy")
    me, count = gx * ngy + gy, ngx * ngy
    fine = Deep(f0, c0, (s0, v0), (ngx, ngy), src.shape, 1.0)
    half_shape = tuple(extent // 2 for extent in src.shape)
    mid = Deep(f1, c1, (s1, v1), (ngx, ngy), half_shape, 4.0)
    fetches = [
        pltpu.make_async_copy(jit, inputs, loads.at[0]),
        pltpu.make_async_copy(lab, labels, loads.at[1]),
        pltpu.make_async_copy(src, held, loads.at[2]),
    ]
    for fetch in fetches:
        fetch.start()
    nx2, ny2 = block.shape[1], block.shape[2]
    big_x, big_y = ngx * nx2, ngy * ny2
    deep = src.shape[2] // 4

    f0[0] = jnp.ones_like(f0.at[0])
    f0[1] = jnp.zeros_like(f0.at[1])
    f1[0] = jnp.ones_like(f1.at[0])
    f1[1] = jnp.zeros_like(f1.at[1])
    grid[...] = jnp.zeros_like(grid)

    def target(offset):
        other = lax.rem(me + offset, count)
        return (lax.div(other, ngy), lax.rem(other, ngy))

    barrier = pltpu.get_barrier_semaphore()

    def greet(offset, carry):
        pl.semaphore_signal(barrier, inc=1, device_id=target(offset), device_id_type=MESH)
        return carry

    lax.fori_loop(1, count, greet, 0)

    fetches[0].wait()
    fetches[1].wait()
    sigma = jnp.where(labels[...] == 1, phase[1], phase[0]) * inputs[...]
    fine.own(0)[...] = sigma
    fetches[2].wait()
    fine.own(1)[...] = held[...]
    pl.semaphore_wait(barrier, count - 1)
    fine.exchange(0, True)
    fine.exchange(1, True)

    def place(kind, x, y):
        return grid.at[kind, pl.ds(1 + x * nx2, nx2), pl.ds(pl.multiple_of(PAD + y * ny2, 8), ny2)]

    def gather_copy(kind, offset, sender):
        return pltpu.make_async_remote_copy(
            src_ref=block.at[kind], dst_ref=place(kind, gx, gy), send_sem=gsend.at[kind],
            recv_sem=grecv.at[kind], device_id=target(offset), device_id_type=MESH,
        )

    def gather_start(kind, values):
        block[kind] = values
        place(kind, gx, gy)[...] = values

        def push(offset, carry):
            gather_copy(kind, offset, me).start()
            return carry

        lax.fori_loop(1, count, push, 0)

    def gather_wait(kind):
        pltpu.make_async_copy(whole, whole, gsend.at[kind]).wait()
        pltpu.make_async_copy(whole, whole, grecv.at[kind]).wait()

    sigma1 = coarsen(sigma, tmp)
    mid.own(0)[...] = sigma1
    mid.exchange(0, True)
    gather_start(0, coarsen(sigma1, tmp))
    fine.exchange(0, False)
    fine.weigh()
    fine.exchange(1, False)

    def mid_weights():
        mid.exchange(0, False)
        mid.weigh()

    chunk = min(big_x, 16)
    rows_y = pl.ds(PAD, big_y)

    def chunks(body):
        if big_x == chunk:
            body(0)
        else:
            def step(index, carry):
                body(index * chunk)
                return carry
            lax.fori_loop(0, big_x // chunk, step, 0)

    def grid_others(kind, first):
        ref = grid.at[kind]
        here = pl.ds(1 + first, chunk)
        centre = ref[here, rows_y, :]
        return centre, [
            ref[pl.ds(2 + first, chunk), rows_y, :], ref[pl.ds(first, chunk), rows_y, :],
            ref[here, pl.ds(PAD + 1, big_y), :], ref[here, pl.ds(PAD - 1, big_y), :],
            pltpu.roll(centre, LANES - 1, 2), pltpu.roll(centre, 1, 2),
        ]

    def coarse_weights():
        gather_wait(0)

        def weigh(first):
            centre, others = grid_others(0, first)
            shape = centre.shape
            at_x, at_y, at_z = (iota(shape, dim) for dim in range(3))
            at_x = at_x + first
            edges = [
                at_x == big_x - 1, at_x == 0, at_y == big_y - 1, at_y == 0,
                lax.rem(at_z, deep) == deep - 1, lax.rem(at_z, deep) == 0,
            ]
            make_coeffs(c2, pl.ds(first, chunk), centre, others, edges, 16.0, None)

        chunks(weigh)

    mid.own(1)[...] = coarsen(fine.smooth(), tmp)
    mid.exchange(1, True)
    out0[...] = fine.own(2)[...]
    mid_weights()
    mid.exchange(1, False)
    gather_start(1, coarsen(mid.smooth(), tmp))
    out1[...] = mid.own(2)[...]
    coarse_weights()
    gather_wait(1)

    def colour(first):
        shape = (chunk, big_y, LANES)
        return lax.rem(iota(shape, 0) + iota(shape, 1) + iota(shape, 2) + first, 2) == 0

    def first_red(first):
        here = pl.ds(first, chunk)
        right = grid[1, pl.ds(1 + first, chunk), rows_y, :] * c2[6, here]
        c2[7, here] = right
        grid[2, pl.ds(1 + first, chunk), rows_y, :] = jnp.where(colour(first), right, 0.0)

    def half(parity):
        def body(first):
            here = pl.ds(first, chunk)
            centre, others = grid_others(2, first)
            fresh = c2[7, here] + linked(c2, here, others)
            red = colour(first)
            turn = red if parity == 0 else jnp.logical_not(red)
            grid[2, pl.ds(1 + first, chunk), rows_y, :] = jnp.where(turn, fresh, centre)
        chunks(body)

    chunks(first_red)
    half(1)

    def sweep(repeat, carry):
        half(0)
        half(1)
        return carry

    lax.fori_loop(0, COARSE_SWEEPS - 1, sweep, 0)
    mine = place(2, gx, gy)[...]
    out2[...] = mine[:, :, :deep]


def per_device(ngx, ngy, source, labels, jitter, phase_sigma):
    nx, ny, nz = source.shape
    count = ngx * ngy
    f32 = jnp.float32

    def deep(nx, ny, nz):
        far = -(-(Deep.REACH + 1) // nx)
        return [
            pltpu.VMEM((3, nx + 2 * far * nx, ny + 2 * PAD, nz), f32),
            pltpu.VMEM((8, nx + 2 * Deep.REACH, ny + 2 * PAD, nz), f32),
            pltpu.SemaphoreType.DMA((2, 6 * far + 2)),
            pltpu.SemaphoreType.DMA((2, 6 * far + 2)),
        ]

    nx2, ny2 = nx // 4, ny // 4
    vmem = pl.BlockSpec(memory_space=pltpu.VMEM)
    hbm = pl.BlockSpec(memory_space=pl.ANY)
    return pl.pallas_call(
        functools.partial(kernel, ngx, ngy),
        out_shape=(
            jax.ShapeDtypeStruct((nx, ny, nz), f32),
            jax.ShapeDtypeStruct((nx // 2, ny // 2, nz // 2), f32),
            jax.ShapeDtypeStruct((nx2, ny2, nz // 4), f32),
        ),
        in_specs=[hbm, hbm, hbm, pl.BlockSpec(memory_space=pltpu.SMEM)],
        out_specs=(vmem, vmem, vmem),
        scratch_shapes=deep(nx, ny, nz) + deep(nx // 2, ny // 2, nz // 2) + [
            pltpu.VMEM((nx, ny, nz), f32),
            pltpu.VMEM((nx, ny, nz), jnp.int32),
            pltpu.VMEM((nx, ny, nz), f32),
            pltpu.SemaphoreType.DMA((3,)),
            pltpu.VMEM((nx // 2 * ny, LANES), f32),
            pltpu.VMEM((2, nx2, ny2, LANES), f32),
            pltpu.VMEM((count - 1, nx2, ny2, LANES), f32),
            pltpu.VMEM((3, ngx * nx2 + 2, ngy * ny2 + 2 * PAD, LANES), f32),
            pltpu.VMEM((8, ngx * nx2, ngy * ny2, LANES), f32),
            pltpu.SemaphoreType.DMA((2,)),
            pltpu.SemaphoreType.DMA((2,)),
        ],
        compiler_params=pltpu.CompilerParams(
            collective_id=0, has_side_effects=True, vmem_limit_bytes=60 * 1024 * 1024
        ),
    )(source, labels, jitter, phase_sigma)


def solution(mesh):
    spec = P("gx", "gy", None)
    return jax.shard_map(
        functools.partial(per_device, mesh.shape["gx"], mesh.shape["gy"]),
        mesh=mesh, in_specs=(spec, spec, spec, P()), out_specs=(spec, spec, spec),
        check_vma=False,
    )
```
